256 devices in a mesh: tm: 32 (over y_hi, z, core), space: 8 (over y_lo, x).
Axes of the slice: x: 4, y: 4 (y_hi: 2, y_lo: 2; y = y_hi * 2 + y_lo), z: 8, core: 2. Of those that a mesh axis runs over, the one named last changes fastest.
Arguments:
- query_tiles: bfloat16 [32, 8, 256, 1536], P('tm', 'space'), may hold values from -6 to 6
- key_tiles: bfloat16 [32, 8, 256, 1536], P('tm', 'space'), may hold values from -6 to 6
- value_tiles: bfloat16 [32, 8, 256, 1536], P('tm', 'space'), may hold values from -6 to 6
- grad_tiles: bfloat16 [32, 8, 256, 1536], P('tm', 'space'), may hold values from -6 to 6
- log_sums: float32 [32, 8, 12, 256], P('tm', 'space'), may hold values from 3 to 5
- row_delta: float32 [32, 8, 12, 256], P('tm', 'space'), may hold values from -24 to 24
- text_keys: bfloat16 [256, 1536], P('space'), may hold values from -6 to 6
- text_values: bfloat16 [256, 1536], P('space'), may hold values from -6 to 6
- touch_list: int32 [32, 8, 128], P('tm', 'space'), may hold values from 0 to 255, as said below
Outputs:
- query_grad: bfloat16 [32, 8, 256, 1536], P('tm', 'space')
- key_grad: bfloat16 [32, 8, 256, 1536], P('tm', 'space')
- value_grad: bfloat16 [32, 8, 256, 1536], P('tm', 'space')
- text_key_grad: bfloat16 [256, 1536], P('space')
- text_value_grad: bfloat16 [256, 1536], P('space')
The draws below stay inside these ranges and needn't reach their ends.
Inputs may be any that keep to these rules, and one draw needn't show every extreme that they name: `touch_list`: every tile's list is the same: the prompt's 128 different non-padding text tokens.
All inputs are finite; a program needn't handle non-finite values.
Results may differ from the reference program's by a relative error of at most 0.006.
Values may be sent and summed in bfloat16 or wider, within the bound.
A program may use at most 128 MiB of HBM per device.

```python
import jax
import jax.numpy as jnp
from jax import lax

HEADS = 12
ROWS = 256
TEXT = 256
TOUCH = 128
TIME_TILES = 32
SPACE_TILES = 8
WIDTH = 1536


def draw_touch_list(key, part):
    key = jax.random.fold_in(key, 7)
    order = jax.random.permutation(key, TEXT)[:TOUCH].astype(jnp.int32)
    return jnp.broadcast_to(order[None, None, :], (TIME_TILES, SPACE_TILES, TOUCH)).astype(jnp.int32)


def block_levels(key, extent, pieces, least, top_value):
    factor_of = 1.0
    for axis_at, parts in pieces:
        draws = jax.random.uniform(jax.random.fold_in(jax.random.fold_in(key, 6), axis_at), (parts,), jnp.float32, least / len(pieces), top_value / len(pieces))
        factor_of = factor_of * jnp.repeat(jnp.exp(draws), extent[axis_at] // parts).reshape((-1,) + (1,) * (len(extent) - 1 - axis_at))
    return factor_of


def gaussian(stream_key, dims, scale, bound, pieces=(), held_as=jnp.bfloat16):
    drawn = scale * jax.random.normal(stream_key, dims, jnp.float32)
    if pieces:
        drawn = drawn * block_levels(stream_key, dims, pieces, -0.22, 0.18)
    return jnp.clip(drawn, -bound, bound).astype(held_as)


def setup_inputs(seed: int = 0) -> dict:
    splits = jax.random.split(jax.random.key(seed), 10)
    query_tiles = gaussian(splits[0], (TIME_TILES, SPACE_TILES, ROWS, WIDTH), 1.0, 6.0, ((0, 32), (1, 8)))
    key_tiles = gaussian(splits[1], (TIME_TILES, SPACE_TILES, ROWS, WIDTH), 1.0, 6.0, ((0, 32), (1, 8)))
    value_tiles = gaussian(splits[2], (TIME_TILES, SPACE_TILES, ROWS, WIDTH), 1.0, 6.0, ((0, 32), (1, 8)))
    grad_tiles = gaussian(splits[3], (TIME_TILES, SPACE_TILES, ROWS, WIDTH), 1.0, 6.0, ((0, 32), (1, 8)))
    log_sums = jnp.clip(3.0 + 2.0 * jax.random.uniform(splits[4], (TIME_TILES, SPACE_TILES, HEADS, ROWS), jnp.float32) ** block_levels(splits[4], (TIME_TILES, SPACE_TILES, HEADS, ROWS), ((0, 32), (1, 8)), -0.2, 0.2), 3.0, 5.0)
    row_delta = gaussian(splits[5], (TIME_TILES, SPACE_TILES, HEADS, ROWS), 4.0, 24.0, ((0, 32), (1, 8)), jnp.float32)
    text_keys = gaussian(splits[6], (TEXT, WIDTH), 1.0, 6.0, ((0, 8),))
    text_values = gaussian(splits[7], (TEXT, WIDTH), 1.0, 6.0, ((0, 8),))
    touch_list = draw_touch_list(jax.random.fold_in(splits[9], 71), 0)
    return {"query_tiles": query_tiles, "key_tiles": key_tiles, "value_tiles": value_tiles, "grad_tiles": grad_tiles, "log_sums": log_sums, "row_delta": row_delta, "text_keys": text_keys, "text_values": text_values, "touch_list": touch_list}


def rounded(values_in):
    return lax.optimization_barrier(values_in.astype(jnp.bfloat16)).astype(jnp.float32)


def block_grads(queries, key_rows, value_rows, grad_rows, saved_sums, saved_delta, retain):
    row_count, feature_width = queries.shape
    head_count = saved_sums.shape[0]
    head_size = feature_width // head_count
    factor = head_size ** -0.5
    query_heads = queries.astype(jnp.float32).reshape(row_count, head_count, head_size)
    key_heads = key_rows.astype(jnp.float32).reshape(-1, head_count, head_size)
    value_heads = value_rows.astype(jnp.float32).reshape(-1, head_count, head_size)
    grad_heads = grad_rows.astype(jnp.float32).reshape(row_count, head_count, head_size)
    scores = jnp.einsum("qhd,khd->hqk", query_heads, key_heads)
    weights = jnp.exp(scores * factor - saved_sums[:, :, None]) * retain
    d_values = jnp.einsum("hqk,qhd->khd", rounded(weights), grad_heads)
    d_weights = jnp.einsum("qhd,khd->hqk", grad_heads, value_heads)
    d_scores = rounded(weights * (d_weights - saved_delta[:, :, None]))
    d_query = jnp.einsum("hqk,khd->qhd", d_scores, key_heads) * factor
    d_keys = jnp.einsum("hqk,qhd->khd", d_scores, query_heads) * factor
    return (d_query.reshape(row_count, feature_width), d_keys.reshape(-1, feature_width), d_values.reshape(-1, feature_width))


def reference(query_tiles, key_tiles, value_tiles, grad_tiles, log_sums, row_delta, text_keys, text_values, touch_list):
    tile_count = query_tiles.shape[0]
    text_count = text_keys.shape[0]
    touched = jnp.any(touch_list[:, :, :, None] == jnp.arange(text_count, dtype=jnp.int32)[None, None, None, :], axis=2).astype(jnp.float32)
    pair_grads = jax.vmap(block_grads, in_axes=(0, 0, 0, 0, 0, 0, None))
    text_grads = jax.vmap(block_grads, in_axes=(0, None, None, 0, 0, 0, 0))
    zeros_tile = jnp.zeros(query_tiles.shape[1:], jnp.float32)
    zeros_text = jnp.zeros(text_keys.shape, jnp.float32)

    def advance(carried, tile_now):
        below_keys, below_values, middle_keys, middle_values, text_dk, text_dv = carried
        earlier = jnp.maximum(tile_now - 1, 0)
        later = jnp.minimum(tile_now + 1, tile_count - 1)
        retain_before = (tile_now >= 1).astype(jnp.float32)
        retain_after = (tile_now + 1 < tile_count).astype(jnp.float32)
        queries = query_tiles[tile_now]
        grads = grad_tiles[tile_now]
        sums_now = log_sums[tile_now]
        delta_now = row_delta[tile_now]
        before = pair_grads(queries, key_tiles[earlier], value_tiles[earlier], grads, sums_now, delta_now, retain_before)
        local = pair_grads(queries, key_tiles[tile_now], value_tiles[tile_now], grads, sums_now, delta_now, jnp.float32(1.0))
        after = pair_grads(queries, key_tiles[later], value_tiles[later], grads, sums_now, delta_now, retain_after)
        textual = text_grads(queries, text_keys, text_values, grads, sums_now, delta_now, touched[tile_now])
        query_sum = rounded(before[0]) + rounded(local[0]) + rounded(after[0]) + rounded(textual[0])
        final_keys = below_keys + rounded(before[1])
        final_values = below_values + rounded(before[2])
        new_state = (middle_keys + rounded(local[1]), middle_values + rounded(local[2]),
                     rounded(after[1]), rounded(after[2]),
                     text_dk + jnp.sum(textual[1], axis=0), text_dv + jnp.sum(textual[2], axis=0))
        return new_state, (query_sum.astype(jnp.bfloat16), final_keys.astype(jnp.bfloat16), final_values.astype(jnp.bfloat16))

    initial = (zeros_tile, zeros_tile, zeros_tile, zeros_tile, zeros_text, zeros_text)
    state, emitted = lax.scan(advance, initial, jnp.arange(tile_count, dtype=jnp.int32))
    key_grad = jnp.concatenate([emitted[1][1:], state[0].astype(jnp.bfloat16)[None]], axis=0)
    value_grad = jnp.concatenate([emitted[2][1:], state[1].astype(jnp.bfloat16)[None]], axis=0)
    return emitted[0], key_grad, value_grad, state[4].astype(jnp.bfloat16), state[5].astype(jnp.bfloat16)
```

```python
import functools
import math

import jax
import jax.numpy as jnp
from jax import lax
from jax.experimental import pallas as pl
from jax.experimental.pallas import tpu as pltpu
from jax.sharding import PartitionSpec as P

MESH = pl.DeviceIdType.MESH
BF16 = jnp.bfloat16
F32 = jnp.float32
HEADS = 12
HEAD = 128
ROWS = 256
WIDTH = HEADS * HEAD
TEXT = 256
TOUCH = 128
SHARD = 32
FACTOR = HEAD**-0.5
LOG2E = math.log2(math.e)
AT_TEXT, AT_PAIR, AT_DQ = 5, 8, 6


def rnd(value):
    return value.astype(BF16).astype(F32)


def dot_nt(a, b):
    return lax.dot_general(a, b, (((1,), (1,)), ((), ())), preferred_element_type=F32)


def dot_nn(a, b):
    return lax.dot_general(a, b, (((1,), (0,)), ((), ())), preferred_element_type=F32)


def pair(queries, grads, sums_row, delta_row, keys, keys_t, values):
    scores = dot_nt(keys, queries)
    weights = jnp.exp2(scores * (FACTOR * LOG2E) - sums_row * LOG2E)
    d_values = dot_nn(weights.astype(BF16), grads)
    d_weights = dot_nt(values, grads)
    d_scores = (weights * (d_weights - delta_row)).astype(BF16)
    d_keys = dot_nn(d_scores, queries) * FACTOR
    d_query = (dot_nn(keys_t, d_scores) * FACTOR).astype(BF16).T
    return d_query, d_keys, d_values


def kernel(
    q_hbm, k_hbm, v_hbm, g_hbm, sums_hbm, delta_hbm, tk_hbm, tv_hbm, touch_hbm,
    dq_out, dk_out, dv_out, tk_out, tv_out,
    tiles, sums, delta, keys_t, k_own, v_own, text, touch,
    dq_acc, dk_acc, dv_acc, dq_sent, dq_back, outs,
    text_f32, text_b16, text_pair, text_sum, plane, plane_sum, z_part, final, wide, text_done,
    load_sem, qg_send, qg_recv, st_send, st_recv, fast_send, fast_recv, dqf_sem, dqs_send, dqs_recv,
    gather_send, gather_recv, fwd_send, fwd_recv, pair_sem, plane_send, plane_recv,
    zr_send, zr_recv, zg_send, zg_recv, done_send, done_recv, out_sem,
):
    t = lax.axis_index("tm")
    s = lax.axis_index("space")
    core = t % 2
    z = (t // 2) % 8
    y_hi = t // 16
    x = s % 4
    y = y_hi * 2 + s // 4
    me = y * 4 + x
    fast = (t + 1 - 2 * core, s)
    slow_t = t - 1 + 2 * core
    has_slow = jnp.logical_and(slow_t >= 0, slow_t < 32)
    slow = (jnp.where(has_slow, slow_t, t), s)
    turn = (x - y + 3) % 4
    active = turn < 3
    my_head = jnp.where(active, 3 * y + turn, 0)

    def chip(place, core_at):
        py, px = place // 4, place % 4
        return (((py // 2) * 8 + z) * 2 + core_at, (py % 2) * 4 + px)

    def along_z(z_at):
        return ((y_hi * 8 + z_at) * 2 + core, s)

    def cols(h):
        return pl.ds(pl.multiple_of(h * HEAD, HEAD), HEAD)

    def rows_of(i, size):
        return pl.ds(pl.multiple_of(i * size, size), size)

    def remote(src, dst, send, recv, device):
        return pltpu.make_async_remote_copy(
            src_ref=src, dst_ref=dst, send_sem=send, recv_sem=recv, device_id=device, device_id_type=MESH
        )

    def loop(count, body):
        lax.fori_loop(0, count, lambda i, c: (body(i), c)[1], 0)

    loads = [
        pltpu.make_async_copy(src, dst, load_sem.at[i])
        for i, (src, dst) in enumerate(
            (
                (q_hbm, tiles.at[0, 0]), (k_hbm, k_own), (g_hbm, tiles.at[0, 1]), (v_hbm, v_own),
                (sums_hbm, sums.at[0]), (delta_hbm, delta.at[0]), (touch_hbm, touch),
                (tk_hbm, text.at[0, rows_of(s, SHARD)]), (tv_hbm, text.at[1, rows_of(s, SHARD)]),
            )
        )
    ]
    for load in loads:
        load.start()

    barrier = pltpu.get_barrier_semaphore()

    def greet_plane(i):
        @pl.when(i != me * 2 + core)
        def _():
            pl.semaphore_signal(barrier, 1, device_id=chip(i // 2, i % 2), device_id_type=MESH)

    def greet_z(i):
        @pl.when(i != z)
        def _():
            pl.semaphore_signal(barrier, 1, device_id=along_z(i), device_id_type=MESH)

    @pl.when(has_slow)
    def _():
        pl.semaphore_signal(barrier, 1, device_id=slow, device_id_type=MESH)

    loop(32, greet_plane)
    loop(8, greet_z)
    pl.semaphore_wait(barrier, 38 + has_slow.astype(jnp.int32))

    def slow_stats(i):
        src, dst = ((sums_hbm, sums.at[2]), (delta_hbm, delta.at[2]))[i]
        return remote(src, dst, st_send.at[i], st_recv.at[i], slow)

    def slow_tile(i, h):
        src = (q_hbm, g_hbm)[i]
        return remote(
            src.at[:, cols(h)], tiles.at[2, i, :, cols(h)], qg_send.at[i, h], qg_recv.at[i, h], slow
        )

    def fast_copy(i):
        src, dst = (
            (sums_hbm, sums.at[1]), (delta_hbm, delta.at[1]), (q_hbm, tiles.at[1, 0]), (g_hbm, tiles.at[1, 1]),
        )[i]
        return remote(src, dst, fast_send.at[i], fast_recv.at[i], fast)

    @pl.when(has_slow)
    def _():
        for i in range(2):
            slow_stats(i).start()

        def send(h):
            slow_tile(0, h).start()
            slow_tile(1, h).start()

        loop(HEADS, send)

    for i in range(4):
        fast_copy(i).start()

    for load in loads[6:]:
        load.wait()

    def gather(i, owner):
        part = text.at[core, rows_of(owner, SHARD)]
        return remote(part, part, gather_send.at[i], gather_recv.at[owner], (t, i))

    def forward(i):
        part = text.at[core, rows_of(i, SHARD)]
        return remote(part, part, fwd_send.at[i], fwd_recv.at[i], fast)

    def forwarded(i):
        part = text.at[1 - core, rows_of(i, SHARD)]
        return remote(part, part, fwd_send.at[i], fwd_recv.at[i], fast)

    def unless(i, own, body):
        @pl.when(i != own)
        def _():
            body()

    loop(8, lambda i: unless(i, s, lambda: gather(i, s).start()))
    for load in loads[:6]:
        load.wait()

    def own_head(h):
        keys = k_own[:, cols(h)]
        turned = keys.T
        keys_t[h] = turned
        dq, dk, dv = pair(
            tiles[0, 0, :, cols(h)], tiles[0, 1, :, cols(h)], sums[0, pl.ds(h, 1), :], delta[0, pl.ds(h, 1), :],
            keys, turned, v_own[:, cols(h)],
        )
        dq_acc[:, cols(h)] = dq.astype(F32)
        dk_acc[:, cols(h)] = rnd(dk)
        dv_acc[:, cols(h)] = rnd(dv)

    loop(HEADS, own_head)

    def near_head(h, slot):
        dq, dk, dv = pair(
            tiles[slot, 0, :, cols(h)], tiles[slot, 1, :, cols(h)],
            sums[slot, pl.ds(h, 1), :], delta[slot, pl.ds(h, 1), :],
            k_own[:, cols(h)], keys_t[h], v_own[:, cols(h)],
        )
        dq_sent[slot - 1, :, cols(h)] = dq
        dk_acc[:, cols(h)] += rnd(dk)
        dv_acc[:, cols(h)] += rnd(dv)

    for i in range(4):
        fast_copy(i).wait_recv()
    loop(HEADS, lambda h: near_head(h, 1))
    dq_fast = remote(dq_sent.at[0], dq_back.at[0], dqf_sem.at[0], dqf_sem.at[1], fast)
    dq_fast.start()

    def hand_over(i):
        gather(i, i).wait_recv()
        forward(i).start()

    loop(8, lambda i: unless(i, s, lambda: hand_over(i)))

    pair_copy = remote(text_b16.at[1 - core], text_pair, pair_sem.at[0], pair_sem.at[1], fast)

    def token_rows():
        token = lax.broadcasted_iota(jnp.int32, (TEXT, TOUCH), 0)
        return jnp.where(token == touch[...], 1.0, 0.0).astype(F32)

    def text_block():
        loop(8, lambda i: unless(i, s, lambda: forwarded(i).wait_recv()))
        pick = token_rows().T.astype(BF16)

        def head(h):
            keys = dot_nn(pick, text[0, :, cols(h)]).astype(BF16)
            values = dot_nn(pick, text[1, :, cols(h)]).astype(BF16)
            dq, dk, dv = pair(
                tiles[0, 0, :, cols(h)], tiles[0, 1, :, cols(h)],
                sums[0, pl.ds(h, 1), :], delta[0, pl.ds(h, 1), :],
                keys, keys.T, values,
            )
            dq_acc[:, cols(h)] += dq.astype(F32)
            text_f32[0, :, cols(h)] = dk
            text_f32[1, :, cols(h)] = dv
            text_b16[0, :, cols(h)] = dk.astype(BF16)
            text_b16[1, :, cols(h)] = dv.astype(BF16)

        loop(HEADS, head)
        pair_copy.start()

    def head_place(h):
        py = h // 3
        return py * 4 + (py + 1 + h % 3) % 4

    def to_plane(h, src):
        return remote(
            text_sum.at[:, cols(h)], plane.at[src], plane_send.at[h], plane_recv.at[src],
            chip(head_place(h), core),
        )

    def pair_sum():
        pair_copy.wait_recv()

        def head(h):
            text_sum[:, cols(h)] = (text_f32[core, :, cols(h)] + text_pair[:, cols(h)].astype(F32)).astype(BF16)

        loop(HEADS, head)
        loop(HEADS, lambda h: unless(head_place(h), me, lambda: to_plane(h, me).start()))

    def dq_slow(h):
        return remote(
            dq_sent.at[1, :, cols(h)], dq_back.at[1, :, cols(h)], dqs_send.at[h], dqs_recv.at[h], slow
        )

    @pl.when(has_slow)
    def _():
        for i in range(2):
            slow_stats(i).wait_recv()

    def slow_head(h):
        pl.when(h == AT_TEXT)(text_block)
        pl.when(h == AT_PAIR)(pair_sum)

        @pl.when(has_slow)
        def _():
            slow_tile(0, h).wait_recv()
            slow_tile(1, h).wait_recv()
            near_head(h, 2)

            @pl.when(h >= AT_DQ)
            def _():
                dq_slow(2 * (h - AT_DQ)).start()
                dq_slow(2 * (h - AT_DQ) + 1).start()

        outs[1, :, cols(h)] = dk_acc[:, cols(h)].astype(BF16)
        outs[2, :, cols(h)] = dv_acc[:, cols(h)].astype(BF16)

    loop(HEADS, slow_head)
    out_copies = [
        pltpu.make_async_copy(outs.at[1], dk_out, out_sem.at[1]),
        pltpu.make_async_copy(outs.at[2], dv_out, out_sem.at[2]),
    ]
    for copy in out_copies:
        copy.start()

    def z_reduce(i, src):
        return remote(
            plane_sum.at[rows_of(i, 16)], z_part.at[src], zr_send.at[i], zr_recv.at[src], along_z(i)
        )

    def z_spread(i, src):
        part = final.at[rows_of(src, 16)]
        return remote(part, part, zg_send.at[i], zg_recv.at[src], along_z(i))

    def deliver(i, head, core_at):
        place = i // 2
        owner = (place // 4 % 2) * 4 + place % 4
        return remote(
            wide.at[rows_of(owner, SHARD)], text_done.at[core_at, :, cols(head)],
            done_send.at[i], done_recv.at[core_at * HEADS + head], chip(place, i % 2),
        )

    @pl.when(active)
    def _():
        plane[me] = text_sum[:, cols(my_head)]
        loop(16, lambda p: unless(p, me, lambda: to_plane(my_head, p).wait_recv()))
        total = plane[0].astype(F32)
        for p in range(1, 16):
            total = total + plane[p].astype(F32)
        plane_sum[...] = total.astype(BF16)
        loop(8, lambda i: unless(i, z, lambda: z_reduce(i, z).start()))
        z_part[z] = plane_sum[rows_of(z, 16), :]
        loop(8, lambda i: unless(i, z, lambda: z_reduce(z, i).wait_recv()))
        total = z_part[0].astype(F32)
        for p in range(1, 8):
            total = total + z_part[p].astype(F32)
        final[rows_of(z, 16), :] = total.astype(BF16)
        loop(8, lambda i: unless(i, z, lambda: z_spread(i, z).start()))
        loop(8, lambda i: unless(i, z, lambda: z_spread(z, i).wait_recv()))
        wide[...] = dot_nn(token_rows().astype(BF16), final[...]).astype(BF16)
        loop(32, lambda i: unless(i, me * 2 + core, lambda: deliver(i, my_head, core).start()))
        text_done[core, :, cols(my_head)] = wide[rows_of(s, SHARD), :]

    dq_fast.wait_recv()

    def finish(h):
        @pl.when(has_slow)
        def _():
            dq_slow(h).wait_recv()

        both = dq_acc[:, cols(h)] + dq_back[0, :, cols(h)].astype(F32)

        @pl.when(has_slow)
        def _():
            outs[0, :, cols(h)] = (both + dq_back[1, :, cols(h)].astype(F32)).astype(BF16)

        @pl.when(jnp.logical_not(has_slow))
        def _():
            outs[0, :, cols(h)] = both.astype(BF16)

    loop(HEADS, finish)
    dq_copy = pltpu.make_async_copy(outs.at[0], dq_out, out_sem.at[0])
    dq_copy.start()

    def done_from(i):
        head, core_at = i % HEADS, i // HEADS
        own = jnp.logical_and(jnp.logical_and(active, head == my_head), core_at == core)

        @pl.when(jnp.logical_not(own))
        def _():
            deliver(me * 2 + core, head, core_at).wait_recv()

    loop(2 * HEADS, done_from)
    text_copies = [
        pltpu.make_async_copy(text_done.at[0], tk_out, out_sem.at[3]),
        pltpu.make_async_copy(text_done.at[1], tv_out, out_sem.at[4]),
    ]
    for copy in text_copies:
        copy.start()

    for i in range(4):
        fast_copy(i).wait_send()
    dq_fast.wait_send()
    pair_copy.wait_send()
    loop(8, lambda i: unless(i, s, lambda: (gather(i, s).wait_send(), forward(i).wait_send())))
    loop(HEADS, lambda h: unless(head_place(h), me, lambda: to_plane(h, me).wait_send()))

    @pl.when(has_slow)
    def _():
        for i in range(2):
            slow_stats(i).wait_send()

        def sent(h):
            slow_tile(0, h).wait_send()
            slow_tile(1, h).wait_send()
            dq_slow(h).wait_send()

        loop(HEADS, sent)

    @pl.when(active)
    def _():
        loop(8, lambda i: unless(i, z, lambda: (z_reduce(i, z).wait_send(), z_spread(i, z).wait_send())))
        loop(32, lambda i: unless(i, me * 2 + core, lambda: deliver(i, my_head, core).wait_send()))

    for copy in out_copies + text_copies + [dq_copy]:
        copy.wait()


def on_device(query_tiles, key_tiles, value_tiles, grad_tiles, log_sums, row_delta, text_keys, text_values, touch_list):
    tile = jax.ShapeDtypeStruct((ROWS, WIDTH), BF16)
    shard = jax.ShapeDtypeStruct((SHARD, WIDTH), BF16)
    dma = pltpu.SemaphoreType.DMA
    dq, dk, dv, tk, tv = pl.pallas_call(
        kernel,
        out_shape=(tile, tile, tile, shard, shard),
        in_specs=[pl.BlockSpec(memory_space=pl.ANY)] * 9,
        out_specs=[pl.BlockSpec(memory_space=pl.ANY)] * 5,
        scratch_shapes=[
            pltpu.VMEM((3, 2, ROWS, WIDTH), BF16),
            pltpu.VMEM((3, HEADS, ROWS), F32),
            pltpu.VMEM((3, HEADS, ROWS), F32),
            pltpu.VMEM((HEADS, HEAD, ROWS), BF16),
            pltpu.VMEM((ROWS, WIDTH), BF16),
            pltpu.VMEM((ROWS, WIDTH), BF16),
            pltpu.VMEM((2, TEXT, WIDTH), BF16),
            pltpu.VMEM((1, TOUCH), jnp.int32),
            pltpu.VMEM((ROWS, WIDTH), F32),
            pltpu.VMEM((ROWS, WIDTH), F32),
            pltpu.VMEM((ROWS, WIDTH), F32),
            pltpu.VMEM((2, ROWS, WIDTH), BF16),
            pltpu.VMEM((2, ROWS, WIDTH), BF16),
            pltpu.VMEM((3, ROWS, WIDTH), BF16),
            pltpu.VMEM((2, TOUCH, WIDTH), F32),
            pltpu.VMEM((2, TOUCH, WIDTH), BF16),
            pltpu.VMEM((TOUCH, WIDTH), BF16),
            pltpu.VMEM((TOUCH, WIDTH), BF16),
            pltpu.VMEM((16, TOUCH, HEAD), BF16),
            pltpu.VMEM((TOUCH, HEAD), BF16),
            pltpu.VMEM((8, 16, HEAD), BF16),
            pltpu.VMEM((TOUCH, HEAD), BF16),
            pltpu.VMEM((TEXT, HEAD), BF16),
            pltpu.VMEM((2, SHARD, WIDTH), BF16),
            dma((9,)),
            dma((2, HEADS)), dma((2, HEADS)),
            dma((2,)), dma((2,)),
            dma((4,)), dma((4,)),
            dma((2,)),
            dma((HEADS,)), dma((HEADS,)),
            dma((8,)), dma((8,)),
            dma((8,)), dma((8,)),
            dma((2,)),
            dma((HEADS,)), dma((16,)),
            dma((8,)), dma((8,)),
            dma((8,)), dma((8,)),
            dma((32,)), dma((2 * HEADS,)),
            dma((5,)),
        ],
        compiler_params=pltpu.CompilerParams(
            collective_id=0, has_side_effects=True, vmem_limit_bytes=60 << 20
        ),
    )(
        query_tiles[0, 0], key_tiles[0, 0], value_tiles[0, 0], grad_tiles[0, 0], log_sums[0, 0], row_delta[0, 0],
        text_keys, text_values, touch_list[0],
    )
    return dq[None, None], dk[None, None], dv[None, None], tk, tv


def solution(mesh):
    tile = P("tm", "space", None, None)
    return jax.shard_map(
        on_device,
        mesh=mesh,
        in_specs=(tile,) * 6 + (P("space", None), P("space", None), P("tm", "space", None)),
        out_specs=(tile, tile, tile, P("space", None), P("space", None)),
        check_vma=False,
    )
```

```python
import functools
import math

import jax
import jax.numpy as jnp
from jax import lax
from jax.experimental import pallas as pl
from jax.experimental.pallas import tpu as pltpu
from jax.sharding import PartitionSpec as P

MESH = pl.DeviceIdType.MESH
BF16 = jnp.bfloat16
F32 = jnp.float32
HEADS = 12
HEAD = 128
ROWS = 256
WIDTH = HEADS * HEAD
TEXT = 256
TOUCH = 128
SHARD = 32
FACTOR = HEAD**-0.5
LOG2E = math.log2(math.e)
GROUP = 4
CHUNK = 2
NEAR = 2
TEXTUAL = 3
TILE = 16
AT_TEXT, AT_PAIR, AT_X = 0, 1, 2


def rnd(value):
    return value.astype(BF16).astype(F32)


def dot_nt(a, b):
    return lax.dot_general(a, b, (((1,), (1,)), ((), ())), preferred_element_type=F32)


def dot_nn(a, b):
    return lax.dot_general(a, b, (((1,), (0,)), ((), ())), preferred_element_type=F32)


def dot_tn(a, b):
    return lax.dot_general(a, b, (((0,), (0,)), ((), ())), preferred_element_type=F32)


def pair(queries, grads, sums_row, delta_row, keys, values):
    scores = dot_nt(keys, queries)
    weights = jnp.exp2(scores * (FACTOR * LOG2E) - sums_row * LOG2E)
    d_values = dot_nn(weights.astype(BF16), grads)
    d_weights = dot_nt(values, grads)
    d_scores = (weights * (d_weights - delta_row)).astype(BF16)
    d_keys = dot_nn(d_scores, queries) * FACTOR
    d_query = (dot_tn(d_scores, keys) * FACTOR).astype(BF16)
    return d_query, d_keys, d_values


def kernel(
    q_hbm, k_hbm, v_hbm, g_hbm, sums_hbm, delta_hbm, tk_hbm, tv_hbm, touch_hbm,
    dq_out, dk_out, dv_out, tk_out, tv_out,
    tiles, sums, delta, k_own, v_own, text, touch,
    dq_acc, dk_acc, dv_acc, dq_sent, dq_back,
    text_f32, text_b16, text_pair, text_sum, x_part, x_sum, tile_part, final, wide, text_done,
    load_sem, qg_send, qg_recv, st_send, st_recv, fast_send, fast_recv, dqf_sem, dqs_send, dqs_recv,
    gather_send, relay_send, gather_recv, fwd_send, fwd_recv, pair_send, pair_recv, x_send, x_recv,
    tile_send, tile_recv, zg_send, zg_recv, done_send, done_recv,
):
    t = lax.axis_index("tm")
    s = lax.axis_index("space")
    core = t % 2
    z = (t // 2) % 8
    y_hi = t // 16
    x = s % 4
    y = y_hi * 2 + s // 4
    me = y * 4 + x
    fast = (t + 1 - 2 * core, s)
    slow_t = t - 1 + 2 * core
    has_slow = jnp.logical_and(slow_t >= 0, slow_t < 32)
    slow = (jnp.where(has_slow, slow_t, t), s)
    far = jnp.logical_or(t == 15, t == 16)
    near = jnp.logical_and(has_slow, jnp.logical_not(far))
    row = s - x
    partner = (s + 4) % 8
    active = y < TEXTUAL
    my_head = jnp.where(active, TEXTUAL * x + y, 0)

    def chip(place, core_at):
        py, px = place // 4, place % 4
        return (((py // 2) * 8 + z) * 2 + core_at, (py % 2) * 4 + px)

    def column(y_at, z_at):
        return (((y_at // 2) * 8 + z_at) * 2 + core, (y_at % 2) * 4 + x)

    def cols(h):
        return pl.ds(pl.multiple_of(h * HEAD, HEAD), HEAD)

    def rows_of(i, size):
        return pl.ds(pl.multiple_of(i * size, size), size)

    def remote(src, dst, send, recv, device):
        return pltpu.make_async_remote_copy(
            src_ref=src, dst_ref=dst, send_sem=send, recv_sem=recv, device_id=device, device_id_type=MESH
        )

    def loop(count, body):
        lax.fori_loop(0, count, lambda i, c: (body(i), c)[1], 0)

    loads = [
        pltpu.make_async_copy(src, dst, load_sem.at[i])
        for i, (src, dst) in enumerate(
            (
                (tk_hbm, text.at[0, rows_of(s, SHARD)]), (tv_hbm, text.at[1, rows_of(s, SHARD)]),
                (q_hbm, tiles.at[0, 0]), (k_hbm, k_own), (g_hbm, tiles.at[0, 1]), (v_hbm, v_own),
                (sums_hbm, sums.at[0]), (delta_hbm, delta.at[0]), (touch_hbm, touch),
            )
        )
    ]
    for load in loads:
        load.start()

    barrier = pltpu.get_barrier_semaphore()

    def greet_plane(i):
        @pl.when(i != me * 2 + core)
        def _():
            pl.semaphore_signal(barrier, 1, device_id=chip(i // 2, i % 2), device_id_type=MESH)

    def greet_column(i):
        @pl.when(i % 8 != z)
        def _():
            pl.semaphore_signal(barrier, 1, device_id=column(i // 8, i % 8), device_id_type=MESH)

    @pl.when(has_slow)
    def _():
        pl.semaphore_signal(barrier, 1, device_id=slow, device_id_type=MESH)

    loop(32, greet_plane)
    loop(32, greet_column)
    pl.semaphore_wait(barrier, 59 + has_slow.astype(jnp.int32))

    def gather(i, owner):
        part = text.at[core, rows_of(owner, SHARD)]
        return remote(part, part, gather_send.at[i], gather_recv.at[owner], (t, i))

    def relay(i, owner):
        part = text.at[core, rows_of(owner, SHARD)]
        return remote(part, part, relay_send.at[i], gather_recv.at[owner], (t, row + i))

    def forward(i):
        part = text.at[core, rows_of(i, SHARD)]
        return remote(part, part, fwd_send.at[i], fwd_recv.at[i], fast)

    def forwarded(i):
        part = text.at[1 - core, rows_of(i, SHARD)]
        return remote(part, part, fwd_send.at[i], fwd_recv.at[i], fast)

    def unless(i, own, body):
        @pl.when(i != own)
        def _():
            body()

    def slow_stats(i):
        src, dst = ((sums_hbm, sums.at[2]), (delta_hbm, delta.at[2]))[i]
        return remote(src, dst, st_send.at[i], st_recv.at[i], slow)

    def slow_tile(i, chunk):
        src = (q_hbm, g_hbm)[i]
        part = pl.ds(pl.multiple_of(chunk * CHUNK * HEAD, CHUNK * HEAD), CHUNK * HEAD)
        return remote(
            src.at[:, part], tiles.at[2, i, :, part], qg_send.at[i, chunk], qg_recv.at[i, chunk], slow
        )

    def fast_copy(i):
        src, dst = (
            (sums_hbm, sums.at[1]), (delta_hbm, delta.at[1]), (q_hbm, tiles.at[1, 0]), (g_hbm, tiles.at[1, 1]),
        )[i]
        return remote(src, dst, fast_send.at[i], fast_recv.at[i], fast)

    for load in loads[:2]:
        load.wait()
    gather(partner, s).start()
    loop(4, lambda i: unless(i, x, lambda: gather(row + i, s).start()))

    def slow_start():
        for i in range(2):
            slow_stats(i).start()

        def send(h):
            slow_tile(0, h).start()
            slow_tile(1, h).start()

        loop(HEADS // CHUNK, send)

    pl.when(near)(slow_start)

    for i in range(4):
        fast_copy(i).start()
    for load in loads[2:]:
        load.wait()

    def heads_of(slot, group, count):
        heads = [group * count + i for i in range(count)]
        return heads, [
            pair(
                tiles[slot, 0, :, cols(h)], tiles[slot, 1, :, cols(h)], sums[slot, h], delta[slot, h],
                k_own[:, cols(h)], v_own[:, cols(h)],
            )
            for h in heads
        ]

    def own_heads(group):
        for h, (dq, dk, dv) in zip(*heads_of(0, group, GROUP)):
            dq_acc[:, cols(h)] = dq.astype(F32)
            dk_acc[:, cols(h)] = rnd(dk)
            dv_acc[:, cols(h)] = rnd(dv)

    loop(HEADS // GROUP, own_heads)
    gather(partner, partner).wait_recv()
    loop(4, lambda i: unless(i, x, lambda: relay(i, partner).start()))
    pl.when(far)(slow_start)

    def near_heads(slot, group, count):
        for h, (dq, dk, dv) in zip(*heads_of(slot, group, count)):
            dq_sent[slot - 1, :, cols(h)] = dq
            dk_acc[:, cols(h)] += rnd(dk)
            dv_acc[:, cols(h)] += rnd(dv)

    for i in range(4):
        fast_copy(i).wait_recv()
    loop(HEADS // GROUP, lambda group: near_heads(1, group, GROUP))
    dq_fast = remote(dq_sent.at[0], dq_back.at[0], dqf_sem.at[0], dqf_sem.at[1], fast)
    dq_fast.start()

    def hand_over(i):
        @pl.when(i != partner)
        def _():
            gather(i, i).wait_recv()

        forward(i).start()

    loop(8, lambda i: unless(i, s, lambda: hand_over(i)))

    def wide_cols(group):
        return pl.ds(pl.multiple_of(group * TEXTUAL * HEAD, TEXTUAL * HEAD), TEXTUAL * HEAD)

    def pair_copy(group):
        return remote(
            text_b16.at[1 - core, :, wide_cols(group)], text_pair.at[:, wide_cols(group)],
            pair_send.at[group], pair_recv.at[group], fast,
        )

    def token_rows():
        token = lax.broadcasted_iota(jnp.int32, (TEXT, TOUCH), 0)
        return jnp.where(token == touch[...], 1.0, 0.0).astype(F32)

    def along_x(i, src):
        return remote(
            text_sum.at[:, wide_cols(i)], x_part.at[src], x_send.at[i], x_recv.at[src], (t, row + i)
        )

    def pair_sum(group):
        pair_copy(group).wait_recv()
        part = wide_cols(group)
        text_sum[:, part] = (text_f32[core, :, part] + text_pair[:, part].astype(F32)).astype(BF16)
        unless(group, x, lambda: along_x(group, x).start())

    def to_owner(i, src):
        return remote(
            x_sum.at[rows_of(i % 8, TILE), cols(i // 8)], tile_part.at[src],
            tile_send.at[i], tile_recv.at[src], column(i // 8, i % 8),
        )

    def x_total():
        loop(4, lambda i: unless(i, x, lambda: along_x(x, i).wait_recv()))
        x_part[x] = text_sum[:, wide_cols(x)]
        total = x_part[0].astype(F32)
        for i in range(1, 4):
            total = total + x_part[i].astype(F32)
        x_sum[...] = total.astype(BF16)
        loop(8 * TEXTUAL, lambda i: unless(i, y * 8 + z, lambda: to_owner(i, y * 8 + z).start()))

    def text_block():
        loop(8, lambda i: unless(i, s, lambda: forwarded(i).wait_recv()))
        pick = token_rows().T.astype(BF16)

        def group_heads(group):
            heads = [group * TEXTUAL + i for i in range(TEXTUAL)]
            keys = [dot_nn(pick, text[0, :, cols(h)]).astype(BF16) for h in heads]
            values = [dot_nn(pick, text[1, :, cols(h)]).astype(BF16) for h in heads]
            terms = [
                pair(tiles[0, 0, :, cols(h)], tiles[0, 1, :, cols(h)], sums[0, h], delta[0, h], keys[i], values[i])
                for i, h in enumerate(heads)
            ]
            for h, (dq, dk, dv) in zip(heads, terms):
                dq_acc[:, cols(h)] += dq.astype(F32)
                text_f32[0, :, cols(h)] = dk
                text_f32[1, :, cols(h)] = dv
                text_b16[0, :, cols(h)] = dk.astype(BF16)
                text_b16[1, :, cols(h)] = dv.astype(BF16)
            pair_copy(group).start()

            @pl.when(group >= 1)
            def _():
                pair_sum(group - 1)

        loop(HEADS // TEXTUAL, group_heads)

    def dq_slow(group):
        part = pl.ds(pl.multiple_of(group * NEAR * HEAD, NEAR * HEAD), NEAR * HEAD)
        return remote(
            dq_sent.at[1, :, part], dq_back.at[1, :, part], dqs_send.at[group], dqs_recv.at[group], slow
        )

    def slow_heads(group):
        pl.when(group == AT_TEXT)(text_block)
        pl.when(group == AT_PAIR)(lambda: pair_sum(HEADS // TEXTUAL - 1))
        pl.when(group == AT_X)(x_total)

        @pl.when(has_slow)
        def _():
            @pl.when(group == 0)
            def _():
                for i in range(2):
                    slow_stats(i).wait_recv()

            @pl.when(group * NEAR % CHUNK == 0)
            def _():
                slow_tile(0, group * NEAR // CHUNK).wait_recv()
                slow_tile(1, group * NEAR // CHUNK).wait_recv()

            near_heads(2, group, NEAR)

            pl.when(near)(lambda: dq_slow(group).start())

        part = pl.ds(pl.multiple_of(group * NEAR * HEAD, NEAR * HEAD), NEAR * HEAD)
        dk_out[:, part] = dk_acc[:, part].astype(BF16)
        dv_out[:, part] = dv_acc[:, part].astype(BF16)

    loop(HEADS // NEAR, slow_heads)

    def z_spread(i, src):
        part = final.at[rows_of(src, TILE)]
        return remote(part, part, zg_send.at[i], zg_recv.at[src], column(y, i))

    def deliver(i, head, core_at):
        place = i // 2
        owner = (place // 4 % 2) * 4 + place % 4
        return remote(
            wide.at[rows_of(owner, SHARD)], text_done.at[core_at, :, cols(head)],
            done_send.at[i], done_recv.at[core_at * HEADS + head], chip(place, i % 2),
        )

    @pl.when(active)
    def _():
        at = y * 8 + z
        tile_part[at] = x_sum[rows_of(z, TILE), cols(y)]
        loop(32, lambda i: unless(i, at, lambda: to_owner(at, i).wait_recv()))
        total = tile_part[0].astype(F32)
        for i in range(1, 32):
            total = total + tile_part[i].astype(F32)
        final[rows_of(z, TILE), :] = total.astype(BF16)
        loop(8, lambda i: unless(i, z, lambda: z_spread(i, z).start()))

    pl.when(far)(lambda: loop(HEADS // NEAR, lambda group: dq_slow(group).start()))

    @pl.when(active)
    def _():
        loop(8, lambda i: unless(i, z, lambda: z_spread(z, i).wait_recv()))
        wide[...] = dot_nn(token_rows().astype(BF16), final[...]).astype(BF16)
        loop(32, lambda i: unless(i, me * 2 + core, lambda: deliver(i, my_head, core).start()))
        text_done[core, :, cols(my_head)] = wide[rows_of(s, SHARD), :]

    dq_fast.wait_recv()

    def finish(group):
        part = pl.ds(pl.multiple_of(group * NEAR * HEAD, NEAR * HEAD), NEAR * HEAD)
        both = dq_acc[:, part] + dq_back[0, :, part].astype(F32)

        @pl.when(has_slow)
        def _():
            dq_slow(group).wait_recv()
            dq_out[:, part] = (both + dq_back[1, :, part].astype(F32)).astype(BF16)

        @pl.when(jnp.logical_not(has_slow))
        def _():
            dq_out[:, part] = both.astype(BF16)

    loop(HEADS // NEAR, finish)

    for i in range(4):
        fast_copy(i).wait_send()
    dq_fast.wait_send()
    loop(HEADS // TEXTUAL, lambda group: pair_copy(group).wait_send())
    gather(partner, s).wait_send()
    loop(8, lambda i: unless(i, s, lambda: forward(i).wait_send()))

    def x_sent(i):
        gather(row + i, s).wait_send()
        relay(i, partner).wait_send()
        along_x(i, x).wait_send()

    loop(4, lambda i: unless(i, x, lambda: x_sent(i)))
    loop(8 * TEXTUAL, lambda i: unless(i, y * 8 + z, lambda: to_owner(i, y * 8 + z).wait_send()))

    @pl.when(has_slow)
    def _():
        for i in range(2):
            slow_stats(i).wait_send()

        def sent(h):
            slow_tile(0, h).wait_send()
            slow_tile(1, h).wait_send()

        loop(HEADS // CHUNK, sent)
        loop(HEADS // NEAR, lambda group: dq_slow(group).wait_send())

    @pl.when(active)
    def _():
        loop(8, lambda i: unless(i, z, lambda: z_spread(i, z).wait_send()))
        loop(32, lambda i: unless(i, me * 2 + core, lambda: deliver(i, my_head, core).wait_send()))

    def done_from(i):
        head, core_at = i % HEADS, i // HEADS
        own = jnp.logical_and(jnp.logical_and(active, head == my_head), core_at == core)

        @pl.when(jnp.logical_not(own))
        def _():
            deliver(me * 2 + core, head, core_at).wait_recv()

    loop(2 * HEADS, done_from)
    tk_out[...] = text_done[0]
    tv_out[...] = text_done[1]


def store(*refs):
    count = (len(refs) - 1) // 2
    copies = [
        pltpu.make_async_copy(refs[i], refs[count + i], refs[-1].at[i]) for i in range(count)
    ]
    for copy in copies:
        copy.start()
    for copy in copies:
        copy.wait()


def on_device(query_tiles, key_tiles, value_tiles, grad_tiles, log_sums, row_delta, text_keys, text_values, touch_list):
    shapes = [(ROWS, WIDTH)] * 3 + [(SHARD, WIDTH)] * 2
    dma = pltpu.SemaphoreType.DMA
    held = pl.pallas_call(
        kernel,
        out_shape=[pltpu.VMEM(shape, BF16) for shape in shapes],
        in_specs=[pl.BlockSpec(memory_space=pl.ANY)] * 9,
        out_specs=[pl.BlockSpec(memory_space=pltpu.VMEM)] * 5,
        scratch_shapes=[
            pltpu.VMEM((3, 2, ROWS, WIDTH), BF16),
            pltpu.VMEM((3, HEADS, 1, ROWS), F32),
            pltpu.VMEM((3, HEADS, 1, ROWS), F32),
            pltpu.VMEM((ROWS, WIDTH), BF16),
            pltpu.VMEM((ROWS, WIDTH), BF16),
            pltpu.VMEM((2, TEXT, WIDTH), BF16),
            pltpu.VMEM((1, TOUCH), jnp.int32),
            pltpu.VMEM((ROWS, WIDTH), F32),
            pltpu.VMEM((ROWS, WIDTH), F32),
            pltpu.VMEM((ROWS, WIDTH), F32),
            pltpu.VMEM((2, ROWS, WIDTH), BF16),
            pltpu.VMEM((2, ROWS, WIDTH), BF16),
            pltpu.VMEM((2, TOUCH, WIDTH), F32),
            pltpu.VMEM((2, TOUCH, WIDTH), BF16),
            pltpu.VMEM((TOUCH, WIDTH), BF16),
            pltpu.VMEM((TOUCH, WIDTH), BF16),
            pltpu.VMEM((4, TOUCH, TEXTUAL * HEAD), BF16),
            pltpu.VMEM((TOUCH, TEXTUAL * HEAD), BF16),
            pltpu.VMEM((32, TILE, HEAD), BF16),
            pltpu.VMEM((TOUCH, HEAD), BF16),
            pltpu.VMEM((TEXT, HEAD), BF16),
            pltpu.VMEM((2, SHARD, WIDTH), BF16),
            dma((9,)),
            dma((2, HEADS)), dma((2, HEADS)),
            dma((2,)), dma((2,)),
            dma((4,)), dma((4,)),
            dma((2,)),
            dma((HEADS // NEAR,)), dma((HEADS // NEAR,)),
            dma((8,)), dma((4,)), dma((8,)),
            dma((8,)), dma((8,)),
            dma((HEADS // TEXTUAL,)), dma((HEADS // TEXTUAL,)),
            dma((4,)), dma((4,)),
            dma((8 * TEXTUAL,)), dma((32,)),
            dma((8,)), dma((8,)),
            dma((32,)), dma((2 * HEADS,)),
        ],
        compiler_params=pltpu.CompilerParams(
            collective_id=0, has_side_effects=True, vmem_limit_bytes=48 << 20
        ),
    )(
        *(
            pltpu.with_memory_space_constraint(value, pltpu.HBM)
            for value in (
                query_tiles[0, 0], key_tiles[0, 0], value_tiles[0, 0], grad_tiles[0, 0],
                log_sums.reshape(HEADS, 1, ROWS), row_delta.reshape(HEADS, 1, ROWS),
                text_keys, text_values, touch_list[0],
            )
        )
    )
    dq, dk, dv, tk, tv = pl.pallas_call(
        store,
        out_shape=[jax.ShapeDtypeStruct(shape, BF16) for shape in shapes],
        in_specs=[pl.BlockSpec(memory_space=pltpu.VMEM)] * 5,
        out_specs=[pl.BlockSpec(memory_space=pl.ANY)] * 5,
        scratch_shapes=[pltpu.SemaphoreType.DMA((5,))],
    )(*(pltpu.with_memory_space_constraint(value, pltpu.VMEM) for value in held))
    return dq[None, None], dk[None, None], dv[None, None], tk, tv


def solution(mesh):
    tile = P("tm", "space", None, None)
    return jax.shard_map(
        on_device,
        mesh=mesh,
        in_specs=(tile,) * 6 + (P("space", None), P("space", None), P("tm", "space", None)),
        out_specs=(tile, tile, tile, P("space", None), P("space", None)),
        check_vma=False,
    )
```

```python
import functools
import math

import jax
import jax.numpy as jnp
from jax import lax
from jax.experimental import pallas as pl
from jax.experimental.pallas import tpu as pltpu
from jax.sharding import PartitionSpec as P

MESH = pl.DeviceIdType.MESH
BF16 = jnp.bfloat16
F32 = jnp.float32
HEADS = 12
HEAD = 128
ROWS = 256
WIDTH = HEADS * HEAD
TEXT = 256
TOUCH = 128
SHARD = 32
FACTOR = HEAD**-0.5
LOG2E = math.log2(math.e)
GROUP = 4
CHUNK = 2
NEAR = 2
TEXTUAL = 3
TILE = 16
AT_TEXT, AT_X, AT_TILE = 0, 1, 4


def rnd(value):
    return value.astype(BF16).astype(F32)


def dot_nt(a, b):
    return lax.dot_general(a, b, (((1,), (1,)), ((), ())), preferred_element_type=F32)


def dot_nn(a, b):
    return lax.dot_general(a, b, (((1,), (0,)), ((), ())), preferred_element_type=F32)


def dot_tn(a, b):
    return lax.dot_general(a, b, (((0,), (0,)), ((), ())), preferred_element_type=F32)


def pair(queries, grads, sums_row, delta_row, keys, values):
    scores = dot_nt(keys, queries)
    weights = jnp.exp2(scores * (FACTOR * LOG2E) - sums_row * LOG2E)
    d_values = dot_nn(weights.astype(BF16), grads)
    d_weights = dot_nt(values, grads)
    d_scores = (weights * (d_weights - delta_row)).astype(BF16)
    d_keys = dot_nn(d_scores, queries) * FACTOR
    d_query = (dot_tn(d_scores, keys) * FACTOR).astype(BF16)
    return d_query, d_keys, d_values


def kernel(
    q_hbm, k_hbm, v_hbm, g_hbm, sums_hbm, delta_hbm, tk_hbm, tv_hbm, touch_hbm,
    dq_out, dk_out, dv_out, tk_out, tv_out,
    tiles, sums, delta, k_own, v_own, text, touch,
    dq_acc, dk_acc, dv_acc, dq_sent, dq_back,
    text_f32, text_b16, text_pair, text_sum, x_part, x_sum, tile_part, final, wide, text_done,
    known, load_sem, text_sem, qg_send, qg_recv, st_send, st_recv, fast_send, fast_recv, dqf_sem, dqs_send, dqs_recv,
    gather_send, gather_recv, fwd_send, fwd_recv, pair_send, pair_recv, x_send, x_recv,
    tile_send, tile_recv, zg_send, zg_recv, done_send, done_recv,
):
    t = lax.axis_index("tm")
    s = lax.axis_index("space")
    core = t % 2
    z = (t // 2) % 8
    y_hi = t // 16
    x = s % 4
    y = y_hi * 2 + s // 4
    me = y * 4 + x
    fast = (t + 1 - 2 * core, s)
    slow_t = t - 1 + 2 * core
    has_slow = jnp.logical_and(slow_t >= 0, slow_t < 32)
    slow = (jnp.where(has_slow, slow_t, t), s)
    far = jnp.logical_or(t == 15, t == 16)
    near = jnp.logical_and(has_slow, jnp.logical_not(far))
    row = s - x
    partner = (s + 4) % 8
    active = y < TEXTUAL
    my_head = jnp.where(active, TEXTUAL * x + y, 0)

    def chip(place, core_at):
        py, px = place // 4, place % 4
        return (((py // 2) * 8 + z) * 2 + core_at, (py % 2) * 4 + px)

    def column(y_at, z_at):
        return (((y_at // 2) * 8 + z_at) * 2 + core, (y_at % 2) * 4 + x)

    def cols(h):
        if isinstance(h, int):
            return pl.ds(h * HEAD, HEAD)
        return pl.ds(pl.multiple_of(h * HEAD, HEAD), HEAD)

    def rows_of(i, size):
        if isinstance(i, int):
            return pl.ds(i * size, size)
        return pl.ds(pl.multiple_of(i * size, size), size)

    def remote(src, dst, send, recv, device):
        return pltpu.make_async_remote_copy(
            src_ref=src, dst_ref=dst, send_sem=send, recv_sem=recv, device_id=device, device_id_type=MESH
        )

    def loop(count, body):
        lax.fori_loop(0, count, lambda i, c: (body(i), c)[1], 0)

    def each(count, body):
        for i in range(count):
            body(i)

    barrier = pltpu.get_barrier_semaphore()
    along_row_at = [(t, row + (x + i) % 4) for i in range(1, 4)]
    beside_y = [column((y + i) % 4, z) for i in (1, 3)]
    beside_z = [column(y, (z + i) % 8) for i in (1, 7)]
    for device in along_row_at + beside_y + beside_z + [fast]:
        pl.semaphore_signal(barrier, 1, device_id=device, device_id_type=MESH)

    @pl.when(has_slow)
    def _():
        pl.semaphore_signal(barrier, 1, device_id=slow, device_id_type=MESH)

    rounds = [beside_z] * 3 + [beside_y] * 2 + [[fast], along_row_at]

    def spread_word(i):
        if i > 0:
            pl.semaphore_wait(known.at[i - 1], len(rounds[i - 1]))
        if i < len(rounds):
            for device in rounds[i]:
                pl.semaphore_signal(known.at[i], 1, device_id=device, device_id_type=MESH)

    loads = [
        pltpu.make_async_copy(src, dst, load_sem.at[i])
        for i, (src, dst) in enumerate(
            (
                (q_hbm, tiles.at[0, 0]), (k_hbm, k_own), (g_hbm, tiles.at[0, 1]), (v_hbm, v_own),
                (sums_hbm, sums.at[0]), (delta_hbm, delta.at[0]), (touch_hbm, touch),
            )
        )
    ]
    own_text = text.at[core, rows_of(s, SHARD)]

    @pl.when(core == 0)
    def _():
        pltpu.make_async_copy(tk_hbm, own_text, text_sem).start()

    @pl.when(core == 1)
    def _():
        pltpu.make_async_copy(tv_hbm, own_text, text_sem).start()

    for load in loads:
        load.start()

    pl.semaphore_wait(barrier, 8 + has_slow.astype(jnp.int32))
    spread_word(0)

    def half(i):
        return pl.ds(i * WIDTH // 2, WIDTH // 2)

    def gather(i, owner, at, sem):
        part = text.at[core, rows_of(owner, SHARD), half(at)]
        return remote(part, part, gather_send.at[sem, at], gather_recv.at[owner, at], (t, i))

    def along_row(i, owner, at):
        return gather(row + i, owner, at, i)

    def relay(i, at):
        return gather(row + i, partner, at, 5 + i)

    def to_partner(owner, at):
        return gather(partner, owner, at, 4)

    def forward(array, first, block, at):
        part = text.at[array, pl.ds(pl.multiple_of(first, 4 * SHARD), 4 * SHARD), half(at)]
        return remote(part, part, fwd_send.at[block, at], fwd_recv.at[block, at], fast)

    def hand_over(at):
        each(4, lambda i: unless(i, x, lambda: along_row(i, row + i, at).wait_recv()))
        forward(core, row * SHARD, 0, at).start()
        each(4, lambda i: unless(i, x, lambda: along_row(i, 4 - row + i, at).wait_recv()))
        forward(core, (4 - row) * SHARD, 1, at).start()

    def handed(at):
        for block, first in enumerate((row, 4 - row)):
            forward(1 - core, first * SHARD, block, at).wait_recv()

    def unless(i, own, body):
        @pl.when(i != own)
        def _():
            body()

    def slow_stats(i):
        src, dst = ((sums_hbm, sums.at[2]), (delta_hbm, delta.at[2]))[i]
        return remote(src, dst, st_send.at[i], st_recv.at[i], slow)

    def slow_tile(i, chunk):
        src = (q_hbm, g_hbm)[i]
        part = pl.ds(pl.multiple_of(chunk * CHUNK * HEAD, CHUNK * HEAD), CHUNK * HEAD)
        return remote(
            src.at[:, part], tiles.at[2, i, :, part], qg_send.at[i, chunk], qg_recv.at[i, chunk], slow
        )

    def fast_copy(i):
        src, dst = (
            (sums_hbm, sums.at[1]), (delta_hbm, delta.at[1]), (q_hbm, tiles.at[1, 0]), (g_hbm, tiles.at[1, 1]),
        )[i]
        return remote(src, dst, fast_send.at[i], fast_recv.at[i], fast)

    pltpu.make_async_copy(tk_hbm, own_text, text_sem).wait()
    for at in range(2):
        to_partner(s, at).start()
        each(4, lambda i: unless(i, x, lambda: along_row(i, s, at).start()))

    def slow_start():
        for i in range(2):
            slow_stats(i).start()

        def send(h):
            slow_tile(0, h).start()
            slow_tile(1, h).start()

        loop(HEADS // CHUNK, send)

    pl.when(near)(slow_start)

    for i in range(4):
        fast_copy(i).start()
    for load in loads:
        load.wait()

    def heads_of(slot, group, count):
        heads = [group * count + i for i in range(count)]
        return heads, [
            pair(
                tiles[slot, 0, :, cols(h)], tiles[slot, 1, :, cols(h)], sums[slot, h], delta[slot, h],
                k_own[:, cols(h)], v_own[:, cols(h)],
            )
            for h in heads
        ]

    def relay_partner():
        for at in range(2):
            to_partner(partner, at).wait_recv()
            each(4, lambda i: unless(i, x, lambda: relay(i, at).start()))
        pl.when(far)(slow_start)

    def own_heads(group):
        pl.when(group == 1)(lambda: spread_word(1))

        @pl.when(group == 2)
        def _():
            spread_word(2)
            relay_partner()

        for h, (dq, dk, dv) in zip(*heads_of(0, group, GROUP)):
            dq_acc[:, cols(h)] = dq.astype(F32)
            dk_acc[:, cols(h)] = rnd(dk)
            dv_acc[:, cols(h)] = rnd(dv)

    loop(HEADS // GROUP, own_heads)

    def near_heads(slot, group, count):
        for h, (dq, dk, dv) in zip(*heads_of(slot, group, count)):
            dq_sent[slot - 1, :, cols(h)] = dq
            dk_acc[:, cols(h)] += rnd(dk)
            dv_acc[:, cols(h)] += rnd(dv)

    for i in range(4):
        fast_copy(i).wait_recv()

    def fast_heads(group):
        for i in range(HEADS // GROUP):
            pl.when(group == i)(lambda i=i: spread_word(3 + i))
        near_heads(1, group, GROUP)

    loop(HEADS // GROUP, fast_heads)
    spread_word(6)
    dq_fast = remote(dq_sent.at[0], dq_back.at[0], dqf_sem.at[0], dqf_sem.at[1], fast)
    dq_fast.start()

    hand_over(0)

    def wide_cols(group):
        return pl.ds(pl.multiple_of(group * TEXTUAL * HEAD, TEXTUAL * HEAD), TEXTUAL * HEAD)

    def pair_copy(group):
        return remote(
            text_b16.at[1 - core, :, wide_cols(group)], text_pair.at[:, wide_cols(group)],
            pair_send.at[group], pair_recv.at[group], fast,
        )

    def token_rows():
        token = lax.broadcasted_iota(jnp.int32, (TEXT, TOUCH), 0)
        return jnp.where(token == touch[...], 1.0, 0.0).astype(F32)

    def along_x(i, src):
        return remote(
            text_sum.at[:, wide_cols(i)], x_part.at[src], x_send.at[i], x_recv.at[src], (t, row + i)
        )

    def pair_sum(group):
        pair_copy(group).wait_recv()
        part = wide_cols(group)
        text_sum[:, part] = (text_f32[core, :, part] + text_pair[:, part].astype(F32)).astype(BF16)

    def group_at(step):
        return (x + 1 + step) % 4

    def to_owner(i, src):
        return remote(
            x_sum.at[rows_of(i % 8, TILE), cols(i // 8)], tile_part.at[src],
            tile_send.at[i], tile_recv.at[src], column(i // 8, i % 8),
        )

    def x_total():
        pair_sum(x)
        each(4, lambda i: unless(i, x, lambda: along_x(x, i).wait_recv()))
        x_part[x] = text_sum[:, wide_cols(x)]
        total = x_part[0].astype(F32)
        for i in range(1, 4):
            total = total + x_part[i].astype(F32)
        x_sum[...] = total.astype(BF16)
        each(8 * TEXTUAL, lambda i: unless(i, y * 8 + z, lambda: to_owner(i, y * 8 + z).start()))

    def text_block():
        pick = token_rows().T.astype(BF16)
        hand_over(1)
        handed(0)
        handed(1)

        def group_heads(step):
            group = group_at(step)
            heads = [group * TEXTUAL + i for i in range(TEXTUAL)]
            keys = [dot_nn(pick, text[0, :, cols(h)]).astype(BF16) for h in heads]
            values = [dot_nn(pick, text[1, :, cols(h)]).astype(BF16) for h in heads]
            terms = [
                pair(tiles[0, 0, :, cols(h)], tiles[0, 1, :, cols(h)], sums[0, h], delta[0, h], keys[i], values[i])
                for i, h in enumerate(heads)
            ]
            for h, (dq, dk, dv) in zip(heads, terms):
                dq_acc[:, cols(h)] += dq.astype(F32)
                text_f32[0, :, cols(h)] = dk
                text_f32[1, :, cols(h)] = dv
                text_b16[0, :, cols(h)] = dk.astype(BF16)
                text_b16[1, :, cols(h)] = dv.astype(BF16)
            pair_copy(group).start()

            @pl.when(step >= 1)
            def _():
                before = group_at(step - 1)
                pair_sum(before)
                along_x(before, x).start()

        loop(HEADS // TEXTUAL, group_heads)

    def z_spread(i, src):
        part = final.at[rows_of(src, TILE)]
        return remote(part, part, zg_send.at[i], zg_recv.at[src], column(y, i))

    def tile_total():
        at = y * 8 + z
        tile_part[at] = x_sum[rows_of(z, TILE), cols(y)]
        each(32, lambda i: unless(i, at, lambda: to_owner(at, i).wait_recv()))
        total = tile_part[0].astype(F32)
        for i in range(1, 32):
            total = total + tile_part[i].astype(F32)
        final[rows_of(z, TILE), :] = total.astype(BF16)
        each(8, lambda i: unless(i, z, lambda: z_spread(i, z).start()))

    def dq_slow(group):
        part = pl.ds(pl.multiple_of(group * NEAR * HEAD, NEAR * HEAD), NEAR * HEAD)
        return remote(
            dq_sent.at[1, :, part], dq_back.at[1, :, part], dqs_send.at[group], dqs_recv.at[group], slow
        )

    def slow_heads(group):
        pl.when(group == AT_TEXT)(text_block)
        pl.when(group == AT_X)(x_total)
        pl.when(jnp.logical_and(active, group == AT_TILE))(tile_total)
        pl.when(jnp.logical_and(far, group == AT_TILE))(
            lambda: loop(AT_TILE, lambda before: dq_slow(before).start())
        )

        @pl.when(has_slow)
        def _():
            @pl.when(group == 0)
            def _():
                for i in range(2):
                    slow_stats(i).wait_recv()

            @pl.when(group * NEAR % CHUNK == 0)
            def _():
                slow_tile(0, group * NEAR // CHUNK).wait_recv()
                slow_tile(1, group * NEAR // CHUNK).wait_recv()

            near_heads(2, group, NEAR)

            pl.when(jnp.logical_or(near, group >= AT_TILE))(lambda: dq_slow(group).start())

        part = pl.ds(pl.multiple_of(group * NEAR * HEAD, NEAR * HEAD), NEAR * HEAD)
        dk_out[:, part] = dk_acc[:, part].astype(BF16)
        dv_out[:, part] = dv_acc[:, part].astype(BF16)

    loop(HEADS // NEAR, slow_heads)

    def deliver(i, head, core_at):
        place = i // 2
        owner = (place // 4 % 2) * 4 + place % 4
        return remote(
            wide.at[rows_of(owner, SHARD)], text_done.at[core_at, :, cols(head)],
            done_send.at[i], done_recv.at[core_at * HEADS + head], chip(place, i % 2),
        )

    @pl.when(active)
    def _():
        each(8, lambda i: unless(i, z, lambda: z_spread(z, i).wait_recv()))
        spread_word(7)
        wide[...] = dot_nn(token_rows().astype(BF16), final[...]).astype(BF16)
        each(32, lambda i: unless(i, me * 2 + core, lambda: deliver(i, my_head, core).start()))
        text_done[core, :, cols(my_head)] = wide[rows_of(s, SHARD), :]

    @pl.when(jnp.logical_not(active))
    def _():
        spread_word(7)

    dq_fast.wait_recv()

    def finish(group):
        part = pl.ds(pl.multiple_of(group * NEAR * HEAD, NEAR * HEAD), NEAR * HEAD)
        both = dq_acc[:, part] + dq_back[0, :, part].astype(F32)

        @pl.when(has_slow)
        def _():
            dq_slow(group).wait_recv()
            dq_out[:, part] = (both + dq_back[1, :, part].astype(F32)).astype(BF16)

        @pl.when(jnp.logical_not(has_slow))
        def _():
            dq_out[:, part] = both.astype(BF16)

    loop(HEADS // NEAR, finish)

    for i in range(4):
        fast_copy(i).wait_send()
    dq_fast.wait_send()
    loop(HEADS // TEXTUAL, lambda group: pair_copy(group).wait_send())
    for at in range(2):
        to_partner(s, at).wait_send()
        for block, first in enumerate((row, 4 - row)):
            forward(core, first * SHARD, block, at).wait_send()

    def x_sent(i):
        for at in range(2):
            along_row(i, s, at).wait_send()
            relay(i, at).wait_send()
        along_x(i, x).wait_send()

    loop(4, lambda i: unless(i, x, lambda: x_sent(i)))
    loop(8 * TEXTUAL, lambda i: unless(i, y * 8 + z, lambda: to_owner(i, y * 8 + z).wait_send()))

    @pl.when(has_slow)
    def _():
        for i in range(2):
            slow_stats(i).wait_send()

        def sent(h):
            slow_tile(0, h).wait_send()
            slow_tile(1, h).wait_send()

        loop(HEADS // CHUNK, sent)
        loop(HEADS // NEAR, lambda group: dq_slow(group).wait_send())

    @pl.when(active)
    def _():
        loop(8, lambda i: unless(i, z, lambda: z_spread(i, z).wait_send()))
        loop(32, lambda i: unless(i, me * 2 + core, lambda: deliver(i, my_head, core).wait_send()))

    def done_from(i):
        head, core_at = i % HEADS, i // HEADS
        own = jnp.logical_and(jnp.logical_and(active, head == my_head), core_at == core)

        @pl.when(jnp.logical_not(own))
        def _():
            deliver(me * 2 + core, head, core_at).wait_recv()

    each(2 * HEADS, done_from)
    tk_out[...] = text_done[0]
    tv_out[...] = text_done[1]


def store(*refs):
    count = (len(refs) - 1) // 2
    copies = [
        pltpu.make_async_copy(refs[i], refs[count + i], refs[-1].at[i]) for i in range(count)
    ]
    for copy in copies:
        copy.start()
    for copy in copies:
        copy.wait()


def on_device(query_tiles, key_tiles, value_tiles, grad_tiles, log_sums, row_delta, text_keys, text_values, touch_list):
    shapes = [(ROWS, WIDTH)] * 3 + [(SHARD, WIDTH)] * 2
    dma = pltpu.SemaphoreType.DMA
    held = pl.pallas_call(
        kernel,
        out_shape=[pltpu.VMEM(shape, BF16) for shape in shapes],
        in_specs=[pl.BlockSpec(memory_space=pl.ANY)] * 9,
        out_specs=[pl.BlockSpec(memory_space=pltpu.VMEM)] * 5,
        scratch_shapes=[
            pltpu.VMEM((3, 2, ROWS, WIDTH), BF16),
            pltpu.VMEM((3, HEADS, 1, ROWS), F32),
            pltpu.VMEM((3, HEADS, 1, ROWS), F32),
            pltpu.VMEM((ROWS, WIDTH), BF16),
            pltpu.VMEM((ROWS, WIDTH), BF16),
            pltpu.VMEM((2, TEXT, WIDTH), BF16),
            pltpu.VMEM((1, TOUCH), jnp.int32),
            pltpu.VMEM((ROWS, WIDTH), F32),
            pltpu.VMEM((ROWS, WIDTH), F32),
            pltpu.VMEM((ROWS, WIDTH), F32),
            pltpu.VMEM((2, ROWS, WIDTH), BF16),
            pltpu.VMEM((2, ROWS, WIDTH), BF16),
            pltpu.VMEM((2, TOUCH, WIDTH), F32),
            pltpu.VMEM((2, TOUCH, WIDTH), BF16),
            pltpu.VMEM((TOUCH, WIDTH), BF16),
            pltpu.VMEM((TOUCH, WIDTH), BF16),
            pltpu.VMEM((4, TOUCH, TEXTUAL * HEAD), BF16),
            pltpu.VMEM((TOUCH, TEXTUAL * HEAD), BF16),
            pltpu.VMEM((32, TILE, HEAD), BF16),
            pltpu.VMEM((TOUCH, HEAD), BF16),
            pltpu.VMEM((TEXT, HEAD), BF16),
            pltpu.VMEM((2, SHARD, WIDTH), BF16),
            pltpu.SemaphoreType.REGULAR((7,)),
            dma((7,)), dma,
            dma((2, HEADS)), dma((2, HEADS)),
            dma((2,)), dma((2,)),
            dma((4,)), dma((4,)),
            dma((2,)),
            dma((HEADS // NEAR,)), dma((HEADS // NEAR,)),
            dma((9, 2)), dma((8, 2)),
            dma((2, 2)), dma((2, 2)),
            dma((HEADS // TEXTUAL,)), dma((HEADS // TEXTUAL,)),
            dma((4,)), dma((4,)),
            dma((8 * TEXTUAL,)), dma((32,)),
            dma((8,)), dma((8,)),
            dma((32,)), dma((2 * HEADS,)),
        ],
        compiler_params=pltpu.CompilerParams(
            collective_id=0, has_side_effects=True, vmem_limit_bytes=48 << 20
        ),
    )(
        *(
            pltpu.with_memory_space_constraint(value, pltpu.HBM)
            for value in (
                query_tiles[0, 0], key_tiles[0, 0], value_tiles[0, 0], grad_tiles[0, 0],
                log_sums.reshape(HEADS, 1, ROWS), row_delta.reshape(HEADS, 1, ROWS),
                text_keys, text_values, touch_list[0],
            )
        )
    )
    dq, dk, dv, tk, tv = pl.pallas_call(
        store,
        out_shape=[jax.ShapeDtypeStruct(shape, BF16) for shape in shapes],
        in_specs=[pl.BlockSpec(memory_space=pltpu.VMEM)] * 5,
        out_specs=[pl.BlockSpec(memory_space=pl.ANY)] * 5,
        scratch_shapes=[pltpu.SemaphoreType.DMA((5,))],
    )(*(pltpu.with_memory_space_constraint(value, pltpu.VMEM) for value in held))
    return dq[None, None], dk[None, None], dv[None, None], tk, tv


def solution(mesh):
    tile = P("tm", "space", None, None)
    return jax.shard_map(
        on_device,
        mesh=mesh,
        in_specs=(tile,) * 6 + (P("space", None), P("space", None), P("tm", "space", None)),
        out_specs=(tile, tile, tile, P("space", None), P("space", None)),
        check_vma=False,
    )
```

```python
import functools
import math

import jax
import jax.numpy as jnp
from jax import lax
from jax.experimental import pallas as pl
from jax.experimental.pallas import tpu as pltpu
from jax.sharding import PartitionSpec as P

MESH = pl.DeviceIdType.MESH
BF16 = jnp.bfloat16
F32 = jnp.float32
HEADS = 12
HEAD = 128
ROWS = 256
WIDTH = HEADS * HEAD
TEXT = 256
TOUCH = 128
SHARD = 32
FACTOR = HEAD**-0.5
LOG2E = math.log2(math.e)
GROUP = 4
CHUNK = 2
NEAR = 2
TEXTUAL = 3
TILE = 16
AT_TEXT, AT_X, AT_TILE = 0, 1, 3


def rnd(value):
    return value.astype(BF16).astype(F32)


def dot_nt(a, b):
    return lax.dot_general(a, b, (((1,), (1,)), ((), ())), preferred_element_type=F32)


def dot_nn(a, b):
    return lax.dot_general(a, b, (((1,), (0,)), ((), ())), preferred_element_type=F32)


def dot_tn(a, b):
    return lax.dot_general(a, b, (((0,), (0,)), ((), ())), preferred_element_type=F32)


def pair(queries, grads, sums_row, delta_row, keys, values):
    scores = dot_nt(keys, queries)
    weights = jnp.exp2(scores * (FACTOR * LOG2E) - sums_row * LOG2E)
    d_values = dot_nn(weights.astype(BF16), grads)
    d_weights = dot_nt(values, grads)
    d_scores = (weights * (d_weights - delta_row)).astype(BF16)
    d_keys = dot_nn(d_scores, queries) * FACTOR
    d_query = (dot_tn(d_scores, keys) * FACTOR).astype(BF16)
    return d_query, d_keys, d_values


def kernel(
    q_hbm, k_hbm, v_hbm, g_hbm, sums_hbm, delta_hbm, tk_hbm, tv_hbm, touch_hbm,
    dq_out, dk_out, dv_out, tk_out, tv_out,
    tiles, sums, delta, k_own, v_own, text, touch,
    dq_acc, dk_acc, dv_acc, dq_sent, dq_back,
    text_f32, text_b16, text_pair, text_sum, x_part, x_sum, tile_part, final, wide, text_done,
    known, load_sem, text_sem, qg_send, qg_recv, st_send, st_recv, fast_send, fast_recv, dqf_sem, dqs_send, dqs_recv,
    gather_send, gather_recv, fwd_send, fwd_recv, pair_send, pair_recv, x_send, x_recv,
    tile_send, tile_recv, zg_send, zg_recv, done_send, done_recv,
):
    t = lax.axis_index("tm")
    s = lax.axis_index("space")
    core = t % 2
    z = (t // 2) % 8
    y_hi = t // 16
    x = s % 4
    y = y_hi * 2 + s // 4
    me = y * 4 + x
    fast = (t + 1 - 2 * core, s)
    slow_t = t - 1 + 2 * core
    has_slow = jnp.logical_and(slow_t >= 0, slow_t < 32)
    slow = (jnp.where(has_slow, slow_t, t), s)
    far = jnp.logical_or(t == 15, t == 16)
    near = jnp.logical_and(has_slow, jnp.logical_not(far))
    row = s - x
    partner = (s + 4) % 8
    active = y < TEXTUAL
    my_head = jnp.where(active, TEXTUAL * x + y, 0)

    def chip(place, core_at):
        py, px = place // 4, place % 4
        return (((py // 2) * 8 + z) * 2 + core_at, (py % 2) * 4 + px)

    def column(y_at, z_at):
        return (((y_at // 2) * 8 + z_at) * 2 + core, (y_at % 2) * 4 + x)

    def cols(h):
        if isinstance(h, int):
            return pl.ds(h * HEAD, HEAD)
        return pl.ds(pl.multiple_of(h * HEAD, HEAD), HEAD)

    def rows_of(i, size):
        if isinstance(i, int):
            return pl.ds(i * size, size)
        return pl.ds(pl.multiple_of(i * size, size), size)

    def remote(src, dst, send, recv, device):
        return pltpu.make_async_remote_copy(
            src_ref=src, dst_ref=dst, send_sem=send, recv_sem=recv, device_id=device, device_id_type=MESH
        )

    def loop(count, body):
        lax.fori_loop(0, count, lambda i, c: (body(i), c)[1], 0)

    def each(count, body):
        for i in range(count):
            body(i)

    barrier = pltpu.get_barrier_semaphore()
    along_row_at = [(t, row + (x + i) % 4) for i in range(1, 4)]
    beside_y = [column((y + i) % 4, z) for i in (1, 3)]
    beside_z = [column(y, (z + i) % 8) for i in (1, 7)]
    for device in along_row_at + beside_y + beside_z + [fast]:
        pl.semaphore_signal(barrier, 1, device_id=device, device_id_type=MESH)

    @pl.when(has_slow)
    def _():
        pl.semaphore_signal(barrier, 1, device_id=slow, device_id_type=MESH)

    rounds = [beside_z] * 3 + [beside_y] * 2 + [[fast], along_row_at]

    def spread_word(i):
        if i > 0:
            pl.semaphore_wait(known.at[i - 1], len(rounds[i - 1]))
        if i < len(rounds):
            for device in rounds[i]:
                pl.semaphore_signal(known.at[i], 1, device_id=device, device_id_type=MESH)

    loads = [
        pltpu.make_async_copy(src, dst, load_sem.at[i])
        for i, (src, dst) in enumerate(
            (
                (q_hbm, tiles.at[0, 0]), (k_hbm, k_own), (g_hbm, tiles.at[0, 1]), (v_hbm, v_own),
                (sums_hbm, sums.at[0]), (delta_hbm, delta.at[0]), (touch_hbm, touch),
            )
        )
    ]
    own_text = text.at[core, rows_of(s, SHARD)]

    @pl.when(core == 0)
    def _():
        pltpu.make_async_copy(tk_hbm, own_text, text_sem).start()

    @pl.when(core == 1)
    def _():
        pltpu.make_async_copy(tv_hbm, own_text, text_sem).start()

    for load in loads:
        load.start()

    pl.semaphore_wait(barrier, 8 + has_slow.astype(jnp.int32))
    spread_word(0)

    def half(i):
        return pl.ds(i * WIDTH // 2, WIDTH // 2)

    def gather(i, owner, at, sem):
        part = text.at[core, rows_of(owner, SHARD), half(at)]
        return remote(part, part, gather_send.at[sem, at], gather_recv.at[owner, at], (t, i))

    def along_row(i, owner, at):
        return gather(row + i, owner, at, i)

    def relay(i, at):
        return gather(row + i, partner, at, 5 + i)

    def to_partner(owner, at):
        return gather(partner, owner, at, 4)

    def forward(array, first, block, at):
        part = text.at[array, pl.ds(pl.multiple_of(first, 4 * SHARD), 4 * SHARD), half(at)]
        return remote(part, part, fwd_send.at[block, at], fwd_recv.at[block, at], fast)

    def hand_over(at):
        each(4, lambda i: unless(i, x, lambda: along_row(i, row + i, at).wait_recv()))
        forward(core, row * SHARD, 0, at).start()
        each(4, lambda i: unless(i, x, lambda: along_row(i, 4 - row + i, at).wait_recv()))
        forward(core, (4 - row) * SHARD, 1, at).start()

    def handed(at):
        for block, first in enumerate((row, 4 - row)):
            forward(1 - core, first * SHARD, block, at).wait_recv()

    def unless(i, own, body):
        @pl.when(i != own)
        def _():
            body()

    def slow_stats(i):
        src, dst = ((sums_hbm, sums.at[2]), (delta_hbm, delta.at[2]))[i]
        return remote(src, dst, st_send.at[i], st_recv.at[i], slow)

    def slow_tile(i, chunk):
        src = (q_hbm, g_hbm)[i]
        part = pl.ds(pl.multiple_of(chunk * CHUNK * HEAD, CHUNK * HEAD), CHUNK * HEAD)
        return remote(
            src.at[:, part], tiles.at[2, i, :, part], qg_send.at[i, chunk], qg_recv.at[i, chunk], slow
        )

    def fast_copy(i):
        src, dst = (
            (sums_hbm, sums.at[1]), (delta_hbm, delta.at[1]), (q_hbm, tiles.at[1, 0]), (g_hbm, tiles.at[1, 1]),
        )[i]
        return remote(src, dst, fast_send.at[i], fast_recv.at[i], fast)

    pltpu.make_async_copy(tk_hbm, own_text, text_sem).wait()
    for at in range(2):
        to_partner(s, at).start()
        each(4, lambda i: unless(i, x, lambda: along_row(i, s, at).start()))

    def slow_start():
        for i in range(2):
            slow_stats(i).start()

        def send(h):
            slow_tile(0, h).start()
            slow_tile(1, h).start()

        loop(HEADS // CHUNK, send)

    pl.when(near)(slow_start)

    for i in range(4):
        fast_copy(i).start()
    for load in loads:
        load.wait()

    def heads_of(slot, group, count):
        heads = [group * count + i for i in range(count)]
        return heads, [
            pair(
                tiles[slot, 0, :, cols(h)], tiles[slot, 1, :, cols(h)], sums[slot, h], delta[slot, h],
                k_own[:, cols(h)], v_own[:, cols(h)],
            )
            for h in heads
        ]

    def relay_partner():
        for at in range(2):
            to_partner(partner, at).wait_recv()
            each(4, lambda i: unless(i, x, lambda: relay(i, at).start()))
        pl.when(far)(slow_start)

    def own_heads(group):
        pl.when(group == 1)(lambda: spread_word(1))

        @pl.when(group == 2)
        def _():
            spread_word(2)
            relay_partner()

        for h, (dq, dk, dv) in zip(*heads_of(0, group, GROUP)):
            dq_acc[:, cols(h)] = dq.astype(F32)
            dk_acc[:, cols(h)] = rnd(dk)
            dv_acc[:, cols(h)] = rnd(dv)

    loop(HEADS // GROUP, own_heads)

    def near_heads(slot, group, count):
        for h, (dq, dk, dv) in zip(*heads_of(slot, group, count)):
            dq_sent[slot - 1, :, cols(h)] = dq
            dk_acc[:, cols(h)] += rnd(dk)
            dv_acc[:, cols(h)] += rnd(dv)

    for i in range(4):
        fast_copy(i).wait_recv()

    def fast_heads(group):
        for i in range(HEADS // GROUP):
            pl.when(group == i)(lambda i=i: spread_word(3 + i))
        near_heads(1, group, GROUP)

    loop(HEADS // GROUP, fast_heads)
    spread_word(6)
    dq_fast = remote(dq_sent.at[0], dq_back.at[0], dqf_sem.at[0], dqf_sem.at[1], fast)
    dq_fast.start()

    hand_over(0)

    def wide_cols(group):
        return pl.ds(pl.multiple_of(group * TEXTUAL * HEAD, TEXTUAL * HEAD), TEXTUAL * HEAD)

    def pair_copy(group):
        return remote(
            text_b16.at[1 - core, :, wide_cols(group)], text_pair.at[:, wide_cols(group)],
            pair_send.at[group], pair_recv.at[group], fast,
        )

    def token_rows():
        token = lax.broadcasted_iota(jnp.int32, (TEXT, TOUCH), 0)
        return jnp.where(token == touch[...], 1.0, 0.0).astype(F32)

    def along_x(i, src):
        return remote(
            text_sum.at[:, wide_cols(i)], x_part.at[src], x_send.at[i], x_recv.at[src], (t, row + i)
        )

    def pair_sum(group):
        pair_copy(group).wait_recv()
        part = wide_cols(group)
        text_sum[:, part] = (text_f32[core, :, part] + text_pair[:, part].astype(F32)).astype(BF16)

    def group_at(step):
        return (x + 1 + step) % 4

    def to_owner(i, src):
        return remote(
            x_sum.at[rows_of(i % 8, TILE), cols(i // 8)], tile_part.at[src],
            tile_send.at[i], tile_recv.at[src], column(i // 8, i % 8),
        )

    def x_total():
        pair_sum(x)
        each(4, lambda i: unless(i, x, lambda: along_x(x, i).wait_recv()))
        x_part[x] = text_sum[:, wide_cols(x)]
        total = x_part[0].astype(F32)
        for i in range(1, 4):
            total = total + x_part[i].astype(F32)
        x_sum[...] = total.astype(BF16)
        each(8 * TEXTUAL, lambda i: unless(i, y * 8 + z, lambda: to_owner(i, y * 8 + z).start()))

    def text_block():
        pick = token_rows().T.astype(BF16)
        hand_over(1)
        handed(0)
        handed(1)

        def group_heads(step):
            group = group_at(step)
            heads = [group * TEXTUAL + i for i in range(TEXTUAL)]
            keys = [dot_nn(pick, text[0, :, cols(h)]).astype(BF16) for h in heads]
            values = [dot_nn(pick, text[1, :, cols(h)]).astype(BF16) for h in heads]
            terms = [
                pair(tiles[0, 0, :, cols(h)], tiles[0, 1, :, cols(h)], sums[0, h], delta[0, h], keys[i], values[i])
                for i, h in enumerate(heads)
            ]
            for h, (dq, dk, dv) in zip(heads, terms):
                dq_acc[:, cols(h)] += dq.astype(F32)
                text_f32[0, :, cols(h)] = dk
                text_f32[1, :, cols(h)] = dv
                text_b16[0, :, cols(h)] = dk.astype(BF16)
                text_b16[1, :, cols(h)] = dv.astype(BF16)
            pair_copy(group).start()

            @pl.when(step >= 1)
            def _():
                before = group_at(step - 1)
                pair_sum(before)
                along_x(before, x).start()

        loop(HEADS // TEXTUAL, group_heads)

    def z_spread(i, src):
        part = final.at[rows_of(src, TILE)]
        return remote(part, part, zg_send.at[i], zg_recv.at[src], column(y, i))

    def tile_total():
        at = y * 8 + z
        tile_part[at] = x_sum[rows_of(z, TILE), cols(y)]
        each(32, lambda i: unless(i, at, lambda: to_owner(at, i).wait_recv()))
        total = tile_part[0].astype(F32)
        for i in range(1, 32):
            total = total + tile_part[i].astype(F32)
        final[rows_of(z, TILE), :] = total.astype(BF16)
        each(8, lambda i: unless(i, z, lambda: z_spread(i, z).start()))

    def dq_slow(group):
        part = pl.ds(pl.multiple_of(group * NEAR * HEAD, NEAR * HEAD), NEAR * HEAD)
        return remote(
            dq_sent.at[1, :, part], dq_back.at[1, :, part], dqs_send.at[group], dqs_recv.at[group], slow
        )

    def slow_heads(group):
        pl.when(group == AT_TEXT)(text_block)
        pl.when(group == AT_X)(x_total)
        pl.when(jnp.logical_and(active, group == AT_TILE))(tile_total)
        pl.when(jnp.logical_and(far, group == AT_TILE))(
            lambda: loop(AT_TILE, lambda before: dq_slow(before).start())
        )

        @pl.when(has_slow)
        def _():
            @pl.when(group == 0)
            def _():
                for i in range(2):
                    slow_stats(i).wait_recv()

            @pl.when(group * NEAR % CHUNK == 0)
            def _():
                slow_tile(0, group * NEAR // CHUNK).wait_recv()
                slow_tile(1, group * NEAR // CHUNK).wait_recv()

            near_heads(2, group, NEAR)

            pl.when(jnp.logical_or(near, group >= AT_TILE))(lambda: dq_slow(group).start())

        part = pl.ds(pl.multiple_of(group * NEAR * HEAD, NEAR * HEAD), NEAR * HEAD)
        dk_out[:, part] = dk_acc[:, part].astype(BF16)
        dv_out[:, part] = dv_acc[:, part].astype(BF16)

    loop(HEADS // NEAR, slow_heads)

    def deliver(i, head, core_at):
        place = i // 2
        owner = (place // 4 % 2) * 4 + place % 4
        return remote(
            wide.at[rows_of(owner, SHARD)], text_done.at[core_at, :, cols(head)],
            done_send.at[i], done_recv.at[core_at * HEADS + head], chip(place, i % 2),
        )

    @pl.when(active)
    def _():
        each(8, lambda i: unless(i, z, lambda: z_spread(z, i).wait_recv()))
        spread_word(7)
        wide[...] = dot_nn(token_rows().astype(BF16), final[...]).astype(BF16)
        each(32, lambda i: unless(i, me * 2 + core, lambda: deliver(i, my_head, core).start()))
        text_done[core, :, cols(my_head)] = wide[rows_of(s, SHARD), :]

    @pl.when(jnp.logical_not(active))
    def _():
        spread_word(7)

    dq_fast.wait_recv()

    def finish(group):
        part = pl.ds(pl.multiple_of(group * NEAR * HEAD, NEAR * HEAD), NEAR * HEAD)
        both = dq_acc[:, part] + dq_back[0, :, part].astype(F32)

        @pl.when(has_slow)
        def _():
            dq_slow(group).wait_recv()
            dq_out[:, part] = (both + dq_back[1, :, part].astype(F32)).astype(BF16)

        @pl.when(jnp.logical_not(has_slow))
        def _():
            dq_out[:, part] = both.astype(BF16)

    loop(HEADS // NEAR, finish)

    for i in range(4):
        fast_copy(i).wait_send()
    dq_fast.wait_send()
    loop(HEADS // TEXTUAL, lambda group: pair_copy(group).wait_send())
    for at in range(2):
        to_partner(s, at).wait_send()
        for block, first in enumerate((row, 4 - row)):
            forward(core, first * SHARD, block, at).wait_send()

    def x_sent(i):
        for at in range(2):
            along_row(i, s, at).wait_send()
            relay(i, at).wait_send()
        along_x(i, x).wait_send()

    loop(4, lambda i: unless(i, x, lambda: x_sent(i)))
    loop(8 * TEXTUAL, lambda i: unless(i, y * 8 + z, lambda: to_owner(i, y * 8 + z).wait_send()))

    @pl.when(has_slow)
    def _():
        for i in range(2):
            slow_stats(i).wait_send()

        def sent(h):
            slow_tile(0, h).wait_send()
            slow_tile(1, h).wait_send()

        loop(HEADS // CHUNK, sent)
        loop(HEADS // NEAR, lambda group: dq_slow(group).wait_send())

    @pl.when(active)
    def _():
        loop(8, lambda i: unless(i, z, lambda: z_spread(i, z).wait_send()))
        loop(32, lambda i: unless(i, me * 2 + core, lambda: deliver(i, my_head, core).wait_send()))

    def done_from(i):
        head, core_at = i % HEADS, i // HEADS
        own = jnp.logical_and(jnp.logical_and(active, head == my_head), core_at == core)

        @pl.when(jnp.logical_not(own))
        def _():
            deliver(me * 2 + core, head, core_at).wait_recv()

    each(2 * HEADS, done_from)
    tk_out[...] = text_done[0]
    tv_out[...] = text_done[1]


def store(*refs):
    count = (len(refs) - 1) // 2
    copies = [
        pltpu.make_async_copy(refs[i], refs[count + i], refs[-1].at[i]) for i in range(count)
    ]
    for copy in copies:
        copy.start()
    for copy in copies:
        copy.wait()


def on_device(query_tiles, key_tiles, value_tiles, grad_tiles, log_sums, row_delta, text_keys, text_values, touch_list):
    shapes = [(ROWS, WIDTH)] * 3 + [(SHARD, WIDTH)] * 2
    dma = pltpu.SemaphoreType.DMA
    held = pl.pallas_call(
        kernel,
        out_shape=[pltpu.VMEM(shape, BF16) for shape in shapes],
        in_specs=[pl.BlockSpec(memory_space=pl.ANY)] * 9,
        out_specs=[pl.BlockSpec(memory_space=pltpu.VMEM)] * 5,
        scratch_shapes=[
            pltpu.VMEM((3, 2, ROWS, WIDTH), BF16),
            pltpu.VMEM((3, HEADS, 1, ROWS), F32),
            pltpu.VMEM((3, HEADS, 1, ROWS), F32),
            pltpu.VMEM((ROWS, WIDTH), BF16),
            pltpu.VMEM((ROWS, WIDTH), BF16),
            pltpu.VMEM((2, TEXT, WIDTH), BF16),
            pltpu.VMEM((1, TOUCH), jnp.int32),
            pltpu.VMEM((ROWS, WIDTH), F32),
            pltpu.VMEM((ROWS, WIDTH), F32),
            pltpu.VMEM((ROWS, WIDTH), F32),
            pltpu.VMEM((2, ROWS, WIDTH), BF16),
            pltpu.VMEM((2, ROWS, WIDTH), BF16),
            pltpu.VMEM((2, TOUCH, WIDTH), F32),
            pltpu.VMEM((2, TOUCH, WIDTH), BF16),
            pltpu.VMEM((TOUCH, WIDTH), BF16),
            pltpu.VMEM((TOUCH, WIDTH), BF16),
            pltpu.VMEM((4, TOUCH, TEXTUAL * HEAD), BF16),
            pltpu.VMEM((TOUCH, TEXTUAL * HEAD), BF16),
            pltpu.VMEM((32, TILE, HEAD), BF16),
            pltpu.VMEM((TOUCH, HEAD), BF16),
            pltpu.VMEM((TEXT, HEAD), BF16),
            pltpu.VMEM((2, SHARD, WIDTH), BF16),
            pltpu.SemaphoreType.REGULAR((7,)),
            dma((7,)), dma,
            dma((2, HEADS)), dma((2, HEADS)),
            dma((2,)), dma((2,)),
            dma((4,)), dma((4,)),
            dma((2,)),
            dma((HEADS // NEAR,)), dma((HEADS // NEAR,)),
            dma((9, 2)), dma((8, 2)),
            dma((2, 2)), dma((2, 2)),
            dma((HEADS // TEXTUAL,)), dma((HEADS // TEXTUAL,)),
            dma((4,)), dma((4,)),
            dma((8 * TEXTUAL,)), dma((32,)),
            dma((8,)), dma((8,)),
            dma((32,)), dma((2 * HEADS,)),
        ],
        compiler_params=pltpu.CompilerParams(
            collective_id=0, has_side_effects=True, vmem_limit_bytes=48 << 20
        ),
    )(
        *(
            pltpu.with_memory_space_constraint(value, pltpu.HBM)
            for value in (
                query_tiles[0, 0], key_tiles[0, 0], value_tiles[0, 0], grad_tiles[0, 0],
                log_sums.reshape(HEADS, 1, ROWS), row_delta.reshape(HEADS, 1, ROWS),
                text_keys, text_values, touch_list[0],
            )
        )
    )
    dq, dk, dv, tk, tv = pl.pallas_call(
        store,
        out_shape=[jax.ShapeDtypeStruct(shape, BF16) for shape in shapes],
        in_specs=[pl.BlockSpec(memory_space=pltpu.VMEM)] * 5,
        out_specs=[pl.BlockSpec(memory_space=pl.ANY)] * 5,
        scratch_shapes=[pltpu.SemaphoreType.DMA((5,))],
    )(*(pltpu.with_memory_space_constraint(value, pltpu.VMEM) for value in held))
    return dq[None, None], dk[None, None], dv[None, None], tk, tv


def solution(mesh):
    tile = P("tm", "space", None, None)
    return jax.shard_map(
        on_device,
        mesh=mesh,
        in_specs=(tile,) * 6 + (P("space", None), P("space", None), P("tm", "space", None)),
        out_specs=(tile, tile, tile, P("space", None), P("space", None)),
        check_vma=False,
    )
```
